256 devices in a mesh: ctx: 32 (over y, z_lo, core), exp: 8 (over z_hi, x).
Axes of the slice: x: 4, y: 4, z: 8 (z_hi: 2, z_lo: 4; z = z_hi * 4 + z_lo), core: 2. Of those that a mesh axis runs over, the one named last changes fastest.
Arguments:
- tokens: bfloat16 [16384, 2048], P(('ctx', 'exp')), may hold values from -6 to 6
- attn_gain: bfloat16 [2048], replicated, may hold values from 0.25 to 1.75
- q_weight: bfloat16 [2048, 4096], P('ctx', 'exp'), may hold values from -0.125 to 0.125
- k_weight: bfloat16 [2048, 512], P('ctx'), may hold values from -0.125 to 0.125
- v_weight: bfloat16 [2048, 512], P('ctx'), may hold values from -0.125 to 0.125
- q_gain: bfloat16 [128], replicated, may hold values from 0.6 to 6, as said below
- k_gain: bfloat16 [128], replicated, may hold values from 0.6 to 6, as said below
- out_weight: bfloat16 [4096, 2048], P('exp', 'ctx'), may hold values from -0.09375 to 0.09375
- moe_gain: bfloat16 [2048], replicated, may hold values from 0.25 to 1.75
- expert_ids: int32 [16384, 2], P(('ctx', 'exp')), may hold values from 0 to 7, all different within a row; in each aligned block of 64 rows (0 to 63, 64 to 127, ...) at most 32 rows name the same one
- route_code: int32 [16384, 2], P(('ctx', 'exp')), may hold values from 1 to 1023
- gate_weight: bfloat16 [8, 2048, 768], P('exp'), may hold values from -0.125 to 0.125
- up_weight: bfloat16 [8, 2048, 768], P('exp'), may hold values from -0.125 to 0.125
- expert_down_matrix: bfloat16 [8, 768, 2048], P('exp'), may hold values from -0.21875 to 0.21875
Outputs:
- layer_out: bfloat16 [16384, 2048], P(('ctx', 'exp'))
The draws below stay inside these ranges and needn't reach their ends.
Inputs may be any that keep to these rules, and one draw needn't show every extreme that they name: `expert_ids`: among the 64 rows of one device no expert is named by more than 32 rows, and in every draw some expert is named by exactly 32 rows of some device. `q_gain`: positive gains. `k_gain`: positive gains.
All inputs are finite; a program needn't handle non-finite values.
Results may differ from the reference program's by a relative error of at most 0.02.
The reference program's roundings to bfloat16 on the way count: a program that leaves them out, or rounds other values in their place, can miss the bound.
Values may be sent and summed in bfloat16 or wider, within the bound.
No kernel may reach another device: no remote copies, remote signals or barrier semaphores. Data moves between devices by JAX's collectives and lax.ppermute only.
A program may use at most 192 MiB of HBM per device.

```python
import math
import jax
import jax.numpy as jnp
import numpy as np
from jax import lax

D = 2048
QH = 32
KVH = 4
HD = 128
FF = 768
TOP = 2
TOK_DEV = 64
EXPERTS = 8
TOKENS = 16384
CAP = 32


def gain_values(key, low, high):
    return jax.random.uniform(key, (HD,), jnp.float32, low, high)


def draw_q_gain(key, part):
    key = jax.random.fold_in(key, 11)
    return gain_values(key, 0.6, 1.6).astype(jnp.bfloat16)


def draw_k_gain(key, part):
    key = jax.random.fold_in(key, 23)
    return gain_values(key, 0.6, 1.6).astype(jnp.bfloat16)


def set_ends(result, stream_key, smallest, top_value):
    spot = [jax.random.randint(jax.random.fold_in(stream_key, axis), (), 0, length) for axis, length in enumerate(result.shape)]
    main_axis = result.shape.index(max(result.shape))
    beside = spot[:main_axis] + [(spot[main_axis] + 1) % result.shape[main_axis]] + spot[main_axis + 1:]
    return result.at[tuple(spot)].set(smallest).at[tuple(beside)].set(top_value)


def level_of(stream_key, dims, shards, low, high):
    def one(axis_at, shards_of):
        heights = jax.random.uniform(jax.random.fold_in(jax.random.fold_in(stream_key, 6), axis_at), (shards_of,), jnp.float32, low / len(shards), high / len(shards))
        return jnp.repeat(jnp.exp(heights), dims[axis_at] // shards_of).reshape((-1,) + (1,) * (len(dims) - axis_at - 1))

    level = one(*shards[0])
    for cut in shards[1:]:
        level = level * one(*cut)
    return level


def deal_out(rng, own, number, rows, count, top, most, skew):
    sequence = jax.random.permutation(rng, count)
    packed, usual = load_shares(count, rows * top, most, skew, True), load_shares(count, rows * top, most, skew, False)
    places = jnp.arange(count)

    def named(lengths, rotation):
        used = int((lengths > 0).sum())
        fixed = max(1, used // 4)
        passed = fixed + (places - fixed + rotation * (used - fixed)) % max(1, count - fixed)
        return jnp.zeros((count,), jnp.int32).at[sequence[jnp.where(places < fixed, places, passed)]].set(jnp.asarray(lengths, jnp.int32))

    lengths = jnp.where(number % 4 == 0, named(packed, number // 4), named(usual, number - number // 4 - 1))
    mixed = jax.random.permutation(jax.random.fold_in(own, 3), count)
    giver, receiver = mixed[0:count // 2 * 2:2], mixed[1:count // 2 * 2:2]
    slack = jnp.minimum(lengths[giver] - 1, most - lengths[receiver]) // 2
    slack = jnp.where((giver == sequence[0]) | (receiver == sequence[0]) | (lengths[receiver] == 0), 0, jnp.maximum(slack, 0))
    passed = jax.random.randint(jax.random.fold_in(own, 4), (count // 2,), 0, 1 << 20) % (slack + 1)
    lengths = lengths.at[giver].add(-passed).at[receiver].add(passed)
    labels = jnp.searchsorted(jnp.cumsum(lengths), jnp.arange(rows * top), side="right").astype(jnp.int32)
    grid = labels.reshape(top, rows).T
    grid = grid[jax.random.permutation(jax.random.fold_in(own, 1), rows)]
    rotation = jax.random.randint(jax.random.fold_in(own, 2), (rows, 1), 0, top)
    return jnp.take_along_axis(grid, (jnp.arange(top)[None, :] + rotation) % top, axis=1)


def load_shares(amount, total, reach, slope, full):
    portions = [(1 << 20) // math.isqrt(grade ** slope) + 1 for grade in range(1, amount + 1)]
    largest = reach if full else min(reach, max(-(-total // amount), total * portions[0] // sum(portions)))
    least = 1 if total - largest >= amount - 1 else 0
    counts, surplus = [largest] + [least] * (amount - 1), total - largest - least * (amount - 1)
    while surplus > 0:
        movable = [i for i in range(1, amount) if counts[i] < largest] or [i for i in range(1, amount) if counts[i] < reach]
        whole, remaining = sum([portions[i] for i in movable]), surplus
        for i in movable:
            addition = min(reach - counts[i], max(1, remaining * portions[i] // whole), surplus)
            counts[i] = counts[i] + addition
            surplus = surplus - addition
    return np.array(counts)


def gaussian(stream_key, shape, spread, bound, shards=(), kind=jnp.bfloat16):
    drawn = jax.random.normal(stream_key, shape, jnp.float32) * spread
    if len(shards) > 0:
        drawn = level_of(stream_key, shape, shards, -0.22, 0.18) * drawn
    return jnp.clip(drawn, min=-bound, max=bound).astype(kind)


def setup_inputs(seed: int = 0) -> dict:
    seeds = jax.random.split(jax.random.key(seed), 15)
    tokens = gaussian(seeds[0], (TOKENS, D), 1.0, 6.0, ((0, 256),))
    attn_gain = jnp.clip(1.0 + 0.15 * jax.random.normal(seeds[1], (D,), jnp.float32), 0.25, 1.75).astype(jnp.bfloat16)
    q_weight = gaussian(seeds[2], (D, QH * HD), D ** -0.5, 0.125, ((0, 32), (1, 8)))
    k_weight = gaussian(seeds[3], (D, KVH * HD), D ** -0.5, 0.125, ((0, 32),))
    v_weight = gaussian(seeds[4], (D, KVH * HD), D ** -0.5, 0.125, ((0, 32),))
    q_gain = draw_q_gain(jax.random.fold_in(seeds[14], 71), 0)
    k_gain = draw_k_gain(jax.random.fold_in(seeds[14], 71), 0)
    out_weight = gaussian(seeds[7], (QH * HD, D), (QH * HD) ** -0.5, 0.09375, ((0, 8), (1, 32)))
    moe_gain = jnp.clip(1.0 + 0.15 * jax.random.normal(seeds[8], (D,), jnp.float32), 0.25, 1.75).astype(jnp.bfloat16)
    expert_ids_keys = jax.random.split(jax.random.fold_in(seeds[9], 1), TOKENS // TOK_DEV)
    expert_ids_turns = jax.random.permutation(jax.random.fold_in(seeds[9], 3), TOKENS // TOK_DEV)
    expert_ids = jax.vmap(lambda own, number: deal_out(jax.random.fold_in(seeds[9], 2), own, number, TOK_DEV, EXPERTS, TOP, CAP, 2))(expert_ids_keys, expert_ids_turns).reshape((TOKENS, TOP))
    route_code = set_ends(jax.random.randint(seeds[10], (TOKENS, TOP), 1, 1024), jax.random.fold_in(seeds[10], 1), 1, 1023).astype(jnp.int32)
    gate_weight = gaussian(seeds[11], (EXPERTS, D, FF), D ** -0.5, 0.125, ((0, 8),))
    up_weight = gaussian(seeds[12], (EXPERTS, D, FF), D ** -0.5, 0.125, ((0, 8),))
    expert_down_matrix = gaussian(seeds[13], (EXPERTS, FF, D), FF ** -0.5, 0.21875, ((0, 8),))
    return {"tokens": tokens, "attn_gain": attn_gain, "q_weight": q_weight, "k_weight": k_weight, "v_weight": v_weight, "q_gain": q_gain, "k_gain": k_gain, "out_weight": out_weight, "moe_gain": moe_gain, "expert_ids": expert_ids, "route_code": route_code, "gate_weight": gate_weight, "up_weight": up_weight, "expert_down_matrix": expert_down_matrix}


def normed(values, gain):
    widened = values.astype(jnp.float32)
    second_expert = lax.optimization_barrier(jnp.mean(widened * widened, axis=-1, keepdims=True))
    return widened * lax.rsqrt(second_expert + 1e-06) * gain.astype(jnp.float32)

def reference(tokens, attn_gain, q_weight, k_weight, v_weight, q_gain, k_gain, out_weight, moe_gain, expert_ids, route_code, gate_weight, up_weight, expert_down_matrix):
    normal_rows = normed(tokens, attn_gain).astype(jnp.bfloat16)
    query_sums = jnp.dot(normal_rows, q_weight, preferred_element_type=jnp.float32)
    queries = normed(query_sums.reshape(TOKENS, QH, HD), q_gain).astype(jnp.bfloat16)
    key_sums = jnp.dot(normal_rows, k_weight, preferred_element_type=jnp.float32)
    keys = normed(key_sums.reshape(TOKENS, KVH, HD), k_gain).astype(jnp.bfloat16)
    values = jnp.dot(normal_rows, v_weight, preferred_element_type=jnp.float32).astype(jnp.bfloat16).reshape(TOKENS, KVH, HD)
    group_size = QH // KVH
    grouped_query_rows = queries.reshape(TOKENS, KVH, group_size, HD)
    block_size = math.gcd(TOKENS, 512)
    block_count = TOKENS // block_size
    key_positions = jnp.arange(TOKENS, dtype=jnp.int32)

    def one_block(index):
        block_index = (index // KVH).astype(jnp.int32)
        head_index = (index % KVH).astype(jnp.int32)
        zero = jnp.zeros((), jnp.int32)
        query_block = lax.dynamic_slice(grouped_query_rows, (block_index * block_size, head_index, zero, zero), (block_size, 1, group_size, HD))[:, 0].astype(jnp.float32)
        key_head = lax.dynamic_index_in_dim(keys, head_index, 1, keepdims=False).astype(jnp.float32)
        value_head = lax.dynamic_index_in_dim(values, head_index, 1, keepdims=False).astype(jnp.float32)
        scores = jnp.einsum('qgd,kd->gqk', query_block, key_head) / math.sqrt(HD)
        query_positions = block_index * block_size + jnp.arange(block_size, dtype=jnp.int32)
        allowed = key_positions[None, :] <= query_positions[:, None]
        masked = jnp.where(allowed[None], scores, -1e+30)
        largest = lax.optimization_barrier(jnp.max(masked, axis=-1, keepdims=True))
        weights = jnp.where(allowed[None], jnp.exp(masked - largest), 0.0)
        denominator = lax.optimization_barrier(jnp.sum(weights, axis=-1, keepdims=True))
        rounded = lax.optimization_barrier(weights.astype(jnp.bfloat16)).astype(jnp.float32)
        return jnp.einsum('gqk,kd->gqd', rounded, value_head) / denominator
    results = lax.map(one_block, jnp.arange(block_count * KVH, dtype=jnp.int32))
    attended = results.reshape(block_count, KVH, group_size, block_size, HD).transpose(0, 3, 1, 2, 4)
    attended = attended.reshape(TOKENS, QH * HD).astype(jnp.bfloat16)
    projected = jnp.dot(attended, out_weight, preferred_element_type=jnp.float32)
    mixed = (tokens.astype(jnp.float32) + projected).astype(jnp.bfloat16)
    moe_in = normed(mixed, moe_gain).astype(jnp.bfloat16)
    codes = route_code.astype(jnp.float32)
    route_weight = codes / lax.optimization_barrier(jnp.sum(codes, axis=-1, keepdims=True))

    def expert_step(carry, inputs):
        gate_one, up_one, down_one, expert_index = inputs
        gate_sums = jnp.dot(moe_in, gate_one, preferred_element_type=jnp.float32)
        up_sums = jnp.dot(moe_in, up_one, preferred_element_type=jnp.float32)
        hidden_state = (jax.nn.silu(gate_sums) * up_sums).astype(jnp.bfloat16)
        expert_out = jnp.dot(hidden_state, down_one, preferred_element_type=jnp.float32).astype(jnp.bfloat16)
        share = lax.optimization_barrier(jnp.sum(jnp.where(expert_ids == expert_index, route_weight, 0.0), axis=-1))
        return (carry + share[:, None] * expert_out.astype(jnp.float32), None)
    initial = jnp.zeros((TOKENS, D), jnp.float32)
    expert_sum, _ = lax.scan(expert_step, initial, (gate_weight, up_weight, expert_down_matrix, jnp.arange(EXPERTS, dtype=jnp.int32)))
    return (mixed.astype(jnp.float32) + expert_sum).astype(jnp.bfloat16)
```

```python
import functools
import math

import jax
import jax.numpy as jnp
from jax import lax
from jax.experimental import pallas as pl
from jax.experimental.pallas import tpu as pltpu
from jax.sharding import PartitionSpec as P

F32 = jnp.float32
BF16 = jnp.bfloat16
NT = (((1,), (1,)), ((), ()))
EPS = 1e-06


def normed(values, gain):
    widened = values.astype(F32)
    square = jnp.mean(widened * widened, axis=-1, keepdims=True)
    return widened * lax.rsqrt(square + EPS) * gain.astype(F32)


def params(vmem_mib):
    return pltpu.CompilerParams(vmem_limit_bytes=vmem_mib * 2**20)


def kv_kernel(place_ref, own_ref, other_ref, w_ref, gain_ref, out_ref):
    half, head = own_ref.shape[0], gain_ref.shape[1]
    mine = place_ref[0]
    for rows_ref, spot in ((own_ref, mine), (other_ref, 1 - mine)):
        sums = jnp.dot(rows_ref[...], w_ref[...], preferred_element_type=F32)
        keys = normed(sums[:, :head], gain_ref[...]).astype(BF16)
        start = pl.multiple_of(spot * half, half)
        out_ref[pl.ds(start, half), :head] = keys
        for part in range(half // head):
            block = sums[part * head : (part + 1) * head, head:]
            out_ref[pl.ds(pl.multiple_of(start + part * head, head), head), head:] = block.T.astype(
                BF16
            )


def q_kernel(place_ref, own_ref, other_ref, w_ref, gain_ref, out_ref):
    head = gain_ref.shape[1]
    mine = place_ref[0]
    for rows_ref, spot in ((own_ref, mine), (other_ref, 1 - mine)):
        sums = jnp.dot(rows_ref[...], w_ref[...], preferred_element_type=F32)
        for one in range(w_ref.shape[1] // head):
            cols = slice(one * head, (one + 1) * head)
            out_ref[spot, :, cols] = normed(sums[:, cols], gain_ref[...]).astype(BF16)


def project(kernel, place, own, other, weights, col_block, width, gain, out_shape):
    half, depth = own.shape
    return pl.pallas_call(
        kernel,
        grid_spec=pltpu.PrefetchScalarGridSpec(
            num_scalar_prefetch=1,
            grid=(1,),
            in_specs=[
                pl.BlockSpec((half, depth), lambda i, p: (0, 0)),
                pl.BlockSpec((half, depth), lambda i, p: (0, 0)),
                pl.BlockSpec((depth, width), lambda i, p: (0, col_block)),
                pl.BlockSpec((1, gain.shape[0]), lambda i, p: (0, 0)),
            ],
            out_specs=pl.BlockSpec(out_shape, lambda i, p: (0,) * len(out_shape)),
        ),
        out_shape=jax.ShapeDtypeStruct(out_shape, BF16),
        compiler_params=params(40),
        cost_estimate=pl.CostEstimate(
            flops=4 * half * depth * width, bytes_accessed=8 * 2**20, transcendentals=0
        ),
    )(place, own, other, weights, gain.reshape(1, -1))


def attention_kernel(scale, place_ref, qa_ref, qb_ref, kv_ref, wo_ref, out_ref, acc_ref, att_ref):
    rows, feats = qa_ref.shape
    head = acc_ref.shape[1]
    heads = feats // head
    block = 2 * rows
    ctx = kv_ref.shape[0] // block
    place = place_ref[0]

    def keys_at(start, count):
        part = kv_ref[pl.ds(pl.multiple_of(start, rows), count), :]
        values = jnp.concatenate(
            [part[i * head : (i + 1) * head, head:] for i in range(count // head)], axis=1
        )
        return part[:, :head], values

    for job, q_ref in ((0, qa_ref), (1, qb_ref)):
        blocks = place if job == 0 else ctx - 1 - place

        def step(start, count, state, first=False, q_ref=q_ref):
            keys, values = keys_at(start, count)
            fresh = []
            for one in range(heads):
                scores = lax.dot_general(
                    keys, q_ref[:, one * head : (one + 1) * head], NT, preferred_element_type=F32
                )
                if first:
                    key_at = lax.broadcasted_iota(jnp.int32, scores.shape, 0)
                    row_at = lax.broadcasted_iota(jnp.int32, scores.shape, 1)
                    scores = jnp.where(key_at <= row_at, scores, -1e30)
                largest = jnp.max(scores, axis=0, keepdims=True)
                if not first:
                    largest = jnp.maximum(largest, state[2 * one])
                weights = jnp.exp2((scores - largest) * scale)
                partial = jnp.sum(weights.reshape(count // 8, 8, rows), axis=0)
                product = lax.dot_general(
                    values,
                    weights.astype(BF16),
                    (((1,), (0,)), ((), ())),
                    preferred_element_type=F32,
                )
                if first:
                    acc_ref[one] = product
                else:
                    decay = jnp.exp2((state[2 * one] - largest) * scale)
                    partial = state[2 * one + 1] * decay + partial
                    acc_ref[one] = acc_ref[one] * decay + product
                fresh += [largest, partial]
            return tuple(fresh)

        state = step(blocks * block + job * rows, rows, None, first=True)
        if job == 1:
            state = step(blocks * block, rows, state)
        state = lax.fori_loop(0, blocks, lambda i, now: step(i * block, block, now), state)
        for one in range(heads):
            total = jnp.sum(state[2 * one + 1], axis=0, keepdims=True)
            att_ref[:, one * head : (one + 1) * head] = (acc_ref[one] / total).T.astype(BF16)
        width = wo_ref.shape[0]
        piece = min(512, width)
        for at in range(0, width, piece):
            out_ref[job, :, at : at + piece] = lax.dot_general(
                att_ref[...], wo_ref[at : at + piece, :], NT, preferred_element_type=F32
            ).astype(BF16)


def attend(place, q_a, q_b, kv, weights, head):
    rows, feats = q_a.shape
    width = weights.shape[0]
    whole = lambda i, p: (0, 0)
    flops = 8 * kv.shape[0] * rows * feats
    return pl.pallas_call(
        functools.partial(attention_kernel, math.log2(math.e) / math.sqrt(head)),
        grid_spec=pltpu.PrefetchScalarGridSpec(
            num_scalar_prefetch=1,
            grid=(1,),
            in_specs=[
                pl.BlockSpec((rows, feats), whole),
                pl.BlockSpec((rows, feats), whole),
                pl.BlockSpec(kv.shape, whole, pipeline_mode=pl.Buffered(1)),
                pl.BlockSpec((width, feats), lambda i, p: (0, 1), pipeline_mode=pl.Buffered(1)),
            ],
            out_specs=pl.BlockSpec((2, rows, width), lambda i, p: (0, 0, 0)),
            scratch_shapes=[
                pltpu.VMEM((feats // head, head, rows), F32),
                pltpu.VMEM((rows, feats), BF16),
            ],
        ),
        out_shape=jax.ShapeDtypeStruct((2, rows, width), BF16),
        compiler_params=params(48),
        cost_estimate=pl.CostEstimate(
            flops=flops, bytes_accessed=16 * 2**20, transcendentals=flops // 256
        ),
    )(place, q_a, q_b, kv, weights)


def shards(
    tokens,
    attn_gain,
    q_weight,
    k_weight,
    v_weight,
    q_gain,
    k_gain,
    out_weight,
    moe_gain,
    expert_ids,
    route_code,
    gate_weight,
    up_weight,
    expert_down_matrix,
):
    exp_count = lax.axis_size("exp")
    ctx_count = lax.axis_size("ctx")
    ctx_place = lax.axis_index("ctx")
    exp_place = lax.axis_index("exp")
    tok_rows, width = tokens.shape
    head = q_gain.shape[0]
    feats = q_weight.shape[1]
    group_size = feats * exp_count // k_weight.shape[1]
    kv_first = exp_place * (feats // head) // group_size * head
    ring = exp_count // 2
    half_rows = tok_rows * ring
    far = exp_place // ring
    near = exp_place % ring
    rings = [list(range(ring)), list(range(ring, exp_count))]
    flip = [(e, (e + ring) % exp_count) for e in range(exp_count)]
    mirror = [(c, ctx_count - 1 - c) for c in range(ctx_count)]

    def over_ring(parts):
        return lax.all_to_all(parts, "exp", 0, 0, tiled=True, axis_index_groups=rings)

    def to_ring(rows):
        spread = jnp.broadcast_to(rows[None], (ring,) + rows.shape)
        return over_ring(spread).reshape(half_rows, width)

    packed = jnp.concatenate(
        [
            q_weight,
            out_weight.T,
            lax.dynamic_slice_in_dim(k_weight, kv_first, head, 1),
            lax.dynamic_slice_in_dim(v_weight, kv_first, head, 1),
        ],
        axis=1,
    )
    weights = lax.all_gather(packed, "ctx", axis=0, tiled=True)
    normal_rows = normed(tokens, attn_gain).astype(BF16)
    flipped = lax.ppermute(normal_rows, "exp", flip)
    own = to_ring(normal_rows)
    other = to_ring(flipped)
    far_index = far.astype(jnp.int32).reshape(1)
    kv = project(
        kv_kernel,
        far_index,
        own,
        other,
        weights,
        feats // head,
        2 * head,
        k_gain,
        (2 * half_rows, 2 * head),
    )
    kv_all = lax.all_gather(kv, "ctx", axis=0, tiled=True)
    queries = project(
        q_kernel, far_index, own, other, weights, 0, feats, q_gain, (2, half_rows, feats)
    )
    mirrored = lax.ppermute(queries[1], "ctx", mirror)
    sums = attend(
        ctx_place.astype(jnp.int32).reshape(1), queries[0], mirrored, kv_all, weights, head
    )
    parts = sums.reshape(2, ring, tok_rows, width).swapaxes(0, 1)
    shares = jnp.sum(over_ring(parts).astype(F32), axis=0)
    rounded = shares.astype(BF16)
    near_half, far_half = range(ring), range(ring, exp_count)
    by_flip = lax.ppermute(rounded[0], "exp", [(e, e - ring) for e in far_half])
    cross = [(c * exp_count + e, (ctx_count - 1 - c) * exp_count + e + ring)
             for c in range(ctx_count) for e in near_half]
    straight = [(c * exp_count + e, (ctx_count - 1 - c) * exp_count + e)
                for c in range(ctx_count) for e in far_half]
    by_cross = lax.ppermute(rounded[1], ("ctx", "exp"), cross)
    by_mirror = lax.ppermute(rounded[1], ("ctx", "exp"), straight)
    head_total = jnp.where(
        far == 0,
        shares[0] + by_flip.astype(F32),
        by_mirror.astype(F32) + by_cross.astype(F32),
    )
    mixed = (tokens.astype(F32) + head_total).astype(BF16)
    moe_in = normed(mixed, moe_gain).astype(BF16)
    top_count = expert_ids.shape[1]
    expert_count = exp_count * gate_weight.shape[0]
    capacity = min(tok_rows, 2 * tok_rows * top_count // expert_count)
    flat_ids = expert_ids.reshape(-1)
    one_hot = (flat_ids[:, None] == jnp.arange(expert_count, dtype=jnp.int32)[None, :]).astype(
        jnp.int32
    )
    earlier = jnp.cumsum(one_hot, axis=0) - one_hot
    slot_rank = jnp.sum(earlier * one_hot, axis=1)
    slots = (flat_ids * capacity + slot_rank).reshape(tok_rows, top_count)
    places = jnp.arange(expert_count * capacity, dtype=jnp.int32)
    selection = jnp.any(places[:, None, None] == slots[None], axis=-1)
    send_rows = jnp.dot(selection.astype(BF16), moe_in, preferred_element_type=F32).astype(BF16)
    send_rows = send_rows.reshape(expert_count, capacity, width)
    codes = route_code.astype(F32)
    route_weight = codes / jnp.sum(codes, axis=-1, keepdims=True)
    arrived = lax.all_to_all(send_rows, "exp", split_axis=0, concat_axis=0, tiled=True)
    flat_rows = arrived.reshape(-1, width)
    gate_sums = jnp.dot(flat_rows, gate_weight[0], preferred_element_type=F32)
    up_sums = jnp.dot(flat_rows, up_weight[0], preferred_element_type=F32)
    hidden = (jax.nn.silu(gate_sums) * up_sums).astype(BF16)
    expert_out = jnp.dot(hidden, expert_down_matrix[0], preferred_element_type=F32).astype(BF16)
    back = lax.all_to_all(
        expert_out.reshape(arrived.shape), "exp", split_axis=0, concat_axis=0, tiled=True
    ).reshape(expert_count * capacity, width)
    total = mixed.astype(F32)
    for j in range(top_count):
        pick = (slots[:, j : j + 1] == places[None, :]).astype(BF16)
        picked = jnp.dot(pick, back, preferred_element_type=F32)
        total = total + picked * route_weight[:, j : j + 1]
    return total.astype(BF16)


def solution(mesh):
    placed = (
        P(("ctx", "exp"), None),
        P(),
        P("ctx", "exp"),
        P("ctx", None),
        P("ctx", None),
        P(),
        P(),
        P("exp", "ctx"),
        P(),
        P(("ctx", "exp"), None),
        P(("ctx", "exp"), None),
        P("exp", None, None),
        P("exp", None, None),
        P("exp", None, None),
    )
    return jax.shard_map(
        shards, mesh=mesh, in_specs=placed, out_specs=P(("ctx", "exp"), None), check_vma=False
    )
```

```python
import functools
import math

import jax
import jax.numpy as jnp
from jax import lax
from jax.experimental import pallas as pl
from jax.experimental.pallas import tpu as pltpu
from jax.sharding import PartitionSpec as P

F32 = jnp.float32
BF16 = jnp.bfloat16
NT = (((1,), (1,)), ((), ()))
EPS = 1e-06


def normed(values, gain):
    widened = values.astype(F32)
    square = jnp.mean(widened * widened, axis=-1, keepdims=True)
    return widened * lax.rsqrt(square + EPS) * gain.astype(F32)


def params(vmem_mib):
    return pltpu.CompilerParams(vmem_limit_bytes=vmem_mib * 2**20)


def in_runs(values, ring):
    run = values.shape[0] // ring
    for job in range(2):
        yield jnp.concatenate(
            [
                values[near * run + job * run // 2 : near * run + (job + 1) * run // 2]
                for near in range(ring)
            ],
            axis=0,
        )


def kv_kernel(ring, place_ref, own_ref, other_ref, w_ref, gain_ref, out_ref):
    half, head = own_ref.shape[0], gain_ref.shape[1]
    mine = place_ref[0]
    for rows_ref, spot in ((own_ref, mine), (other_ref, 1 - mine)):
        sums = jnp.dot(rows_ref[...], w_ref[...], preferred_element_type=F32)
        for job, part in enumerate(in_runs(sums, ring)):
            keys = normed(part[:, :head], gain_ref[...]).astype(BF16)
            start = job * half + pl.multiple_of(spot * (half // 2), half // 2)
            out_ref[pl.ds(start, half // 2), :head] = keys
            for at in range(0, half // 2, head):
                block = part[at : at + head, head:].T.astype(BF16)
                out_ref[pl.ds(start + at, head), head:] = block


def q_kernel(ring, place_ref, own_ref, other_ref, w_ref, gain_ref, out_ref):
    half, head = own_ref.shape[0], gain_ref.shape[1]
    mine = place_ref[0]
    for rows_ref, spot in ((own_ref, mine), (other_ref, 1 - mine)):
        sums = jnp.dot(rows_ref[...], w_ref[...], preferred_element_type=F32)
        for job, part in enumerate(in_runs(sums, ring)):
            start = pl.multiple_of(spot * (half // 2), half // 2)
            for one in range(w_ref.shape[1] // head):
                cols = slice(one * head, (one + 1) * head)
                out_ref[job, pl.ds(start, half // 2), cols] = normed(
                    part[:, cols], gain_ref[...]
                ).astype(BF16)


def project(kernel, ring, place, own, other, weights, col_block, width, gain, out_shape):
    half, depth = own.shape
    return pl.pallas_call(
        functools.partial(kernel, ring),
        grid_spec=pltpu.PrefetchScalarGridSpec(
            num_scalar_prefetch=1,
            grid=(1,),
            in_specs=[
                pl.BlockSpec((half, depth), lambda i, p: (0, 0)),
                pl.BlockSpec((half, depth), lambda i, p: (0, 0)),
                pl.BlockSpec((depth, width), lambda i, p: (0, col_block)),
                pl.BlockSpec((1, gain.shape[0]), lambda i, p: (0, 0)),
            ],
            out_specs=pl.BlockSpec(out_shape, lambda i, p: (0,) * len(out_shape)),
        ),
        out_shape=jax.ShapeDtypeStruct(out_shape, BF16),
        compiler_params=params(40),
        cost_estimate=pl.CostEstimate(
            flops=4 * half * depth * width, bytes_accessed=8 * 2**20, transcendentals=0
        ),
    )(place, own, other, weights, gain.reshape(1, -1))


def attention_kernel(
    scale, part, place_ref, q_ref, kv_hbm, w_hbm, out_ref, kv_ref, wo_ref, qt_ref, acc_ref, att_ref, sems, wo_sem
):
    ring, jobs, sides, tile, width = out_ref.shape
    half, feats = q_ref.shape[1:]
    head = acc_ref.shape[0]
    heads = feats // head
    devices = ring * sides
    rows = devices * tile
    span = half // devices
    block = 2 * half
    chunks = sems.shape[0]
    ctx = kv_ref.shape[0] // block
    per = ctx // chunks
    place = place_ref[0]
    pair = 2
    cols = pair * rows
    longest = jnp.maximum(place, ctx - 1 - place)

    def chunk_wait(at):
        piece = pl.ds(pl.multiple_of(at * per * block, block), per * block)
        pltpu.make_async_copy(kv_hbm.at[piece], kv_ref.at[piece], sems.at[at]).wait()

    wo_copy = pltpu.make_async_copy(w_hbm.at[:, feats : 2 * feats], wo_ref, wo_sem)
    for at in range(chunks):
        @pl.when(at * per <= longest)
        def _(at=at):
            for one in range(at * per, (at + 1) * per):
                first = pl.ds(one * block, half)
                pltpu.make_async_copy(kv_hbm.at[first], kv_ref.at[first], sems.at[at]).start()
                pltpu.make_async_copy(
                    kv_hbm.at[pl.ds((ctx - 1 - one) * block + half, half)],
                    kv_ref.at[pl.ds(one * block + half, half)],
                    sems.at[at],
                ).start()

    wo_copy.start()

    for job in range(2):
        for one in range(heads):
            picked = jnp.concatenate(
                [
                    q_ref[
                        job,
                        e * span + part * tile : e * span + (part + 1) * tile,
                        one * head : (one + 1) * head,
                    ]
                    for e in range(devices)
                ],
                axis=0,
            )
            qt_ref[job, :, one * rows : (one + 1) * rows] = picked.astype(F32).T.astype(BF16)

    def one_job(turn, carry):
        own = jnp.where(turn == 0, place >= ctx - 1 - place, place < ctx - 1 - place)
        job = jnp.where(own, 0, 1)
        blocks = jnp.where(own, place, ctx - 1 - place)
        groups = heads // pair

        def steps(starts, count, state, masked=False):
            state = list(state)
            items = [(start, group) for start in starts for group in range(groups)]

            def product(item):
                start, group = item
                keys = kv_ref[pl.ds(pl.multiple_of(start, half), count), :head]
                queries = qt_ref[job, :, group * cols : (group + 1) * cols]
                return jnp.dot(keys, queries, preferred_element_type=F32)

            def collect(start, group, weights, decay):
                values = jnp.concatenate(
                    [
                        kv_ref[pl.ds(pl.multiple_of(start + i * head, head), head), head:]
                        for i in range(count // head)
                    ],
                    axis=1,
                )
                spot = slice(group * cols, (group + 1) * cols)
                acc_ref[:, spot] = acc_ref[:, spot] * decay + jnp.dot(
                    values, weights, preferred_element_type=F32
                )

            following = product(items[0])
            waiting = None
            for at, (start, group) in enumerate(items):
                scores = following
                if at + 1 < len(items):
                    following = product(items[at + 1])
                if masked:
                    key_at = lax.broadcasted_iota(jnp.int32, scores.shape, 0)
                    col = lax.broadcasted_iota(jnp.int32, scores.shape, 1) % rows
                    row_at = (col // tile * 2 + job) * span + part * tile + col % tile
                    key_at = (key_at % half // span * 2 + key_at // half) * span + key_at % span
                    scores = jnp.where(key_at <= row_at, scores, -1e30)
                before, total = state[2 * group], state[2 * group + 1]
                largest = jnp.maximum(before, jnp.max(scores, axis=0, keepdims=True))
                weights = jnp.exp2((scores - largest) * scale)
                decay = jnp.exp2((before - largest) * scale)
                state[2 * group] = largest
                state[2 * group + 1] = total * decay + jnp.sum(
                    weights.reshape(count // 8, 8, cols), axis=0
                )
                if waiting is not None:
                    collect(*waiting)
                waiting = (start, group, weights.astype(BF16), decay)
            collect(*waiting)
            return tuple(state)

        def arrive(at):
            @pl.when(turn == 0)
            def _():
                chunk_wait(at)

        def whole_chunk(at, state):
            arrive(at)
            return steps([(at * per + i) * block for i in range(per)], block, state)

        acc_ref[...] = jnp.zeros_like(acc_ref)
        state = (jnp.full((1, cols), -1e30, F32), jnp.zeros((8, cols), F32)) * groups
        full = blocks // per
        state = lax.fori_loop(0, full, whole_chunk, state)
        arrive(full)
        state = lax.fori_loop(
            full * per, blocks, lambda i, now: steps([i * block], block, now), state
        )
        state = steps([blocks * block], block, state, masked=True)
        for group in range(groups):
            total = jnp.sum(state[2 * group + 1], axis=0, keepdims=True)
            spot = slice(group * cols, (group + 1) * cols)
            acc_ref[:, spot] = acc_ref[:, spot] / total
        for one in range(heads):
            att_ref[:, one * head : (one + 1) * head] = acc_ref[
                :, one * rows : (one + 1) * rows
            ].T.astype(BF16)

        @pl.when(turn == 0)
        def _():
            wo_copy.wait()

        piece = min(512, width)
        for at in range(0, width, piece):
            sums = lax.dot_general(
                att_ref[...], wo_ref[at : at + piece, :], NT, preferred_element_type=F32
            ).astype(BF16)
            for e in range(devices):
                out_ref[e % ring, job, e // ring, :, at : at + piece] = sums[
                    e * tile : (e + 1) * tile
                ]
        return carry

    lax.fori_loop(0, 2, one_job, 0)


def attend(place, queries, kv, weights, head, ring, part, parts):
    half, feats = queries.shape[1:]
    width = weights.shape[0]
    tile = half // (2 * ring) // parts
    rows = tile * 2 * ring
    ctx = kv.shape[0] // (2 * half)
    chunks = max(1, ctx // 4)
    flops = 8 * kv.shape[0] * rows * feats
    return pl.pallas_call(
        functools.partial(attention_kernel, math.log2(math.e) / math.sqrt(head), part),
        grid_spec=pltpu.PrefetchScalarGridSpec(
            num_scalar_prefetch=1,
            grid=(1,),
            in_specs=[
                pl.BlockSpec((2, half, feats), lambda i, p: (0, 0, 0)),
                pl.BlockSpec(memory_space=pltpu.HBM),
                pl.BlockSpec(memory_space=pltpu.HBM),
            ],
            out_specs=pl.BlockSpec((ring, 2, 2, tile, width), lambda i, p: (0,) * 5),
            scratch_shapes=[
                pltpu.VMEM(kv.shape, BF16),
                pltpu.VMEM((width, feats), BF16),
                pltpu.VMEM((2, head, rows * feats // head), BF16),
                pltpu.VMEM((head, rows * feats // head), F32),
                pltpu.VMEM((rows, feats), BF16),
                pltpu.SemaphoreType.DMA((chunks,)),
                pltpu.SemaphoreType.DMA,
            ],
        ),
        out_shape=jax.ShapeDtypeStruct((ring, 2, 2, tile, width), BF16),
        compiler_params=params(58),
        cost_estimate=pl.CostEstimate(
            flops=flops, bytes_accessed=16 * 2**20, transcendentals=flops // 512
        ),
    )(place, queries, kv, weights)


def mix_kernel(tokens_ref, kept_ref, flip_ref, mirror_ref, cross_ref, gain_ref, chosen_ref, mixed_ref, sent_ref):
    half = kept_ref.shape[0]
    own = kept_ref[...] + flip_ref[...].astype(F32)
    others = mirror_ref[...].astype(F32) + cross_ref[...].astype(F32)
    mixed_ref[:half] = (tokens_ref[:half].astype(F32) + own).astype(BF16)
    mixed_ref[half:] = (tokens_ref[half:].astype(F32) + others).astype(BF16)
    rows = normed(mixed_ref[...], gain_ref[...]).astype(BF16)
    sent_ref[...] = jnp.dot(chosen_ref[...], rows, preferred_element_type=F32).astype(BF16)


def expert_kernel(rows_ref, gate_ref, up_ref, down_ref, out_ref, total_ref):
    step = pl.program_id(0)
    gate = jnp.dot(rows_ref[...], gate_ref[...], preferred_element_type=F32)
    up = jnp.dot(rows_ref[...], up_ref[...], preferred_element_type=F32)
    hidden = (gate / (1.0 + jnp.exp(-gate)) * up).astype(BF16)
    share = jnp.dot(hidden, down_ref[...], preferred_element_type=F32)

    @pl.when(step == 0)
    def _():
        total_ref[...] = share

    @pl.when(step > 0)
    def _():
        total_ref[...] += share

    @pl.when(step == pl.num_programs(0) - 1)
    def _():
        out_ref[...] = total_ref[...].astype(BF16)


def run_experts(rows, gate_weight, up_weight, down_weight):
    count, width = rows.shape
    inner = gate_weight.shape[1]
    piece = math.gcd(inner, 256)
    return pl.pallas_call(
        expert_kernel,
        grid=(inner // piece,),
        in_specs=[
            pl.BlockSpec((count, width), lambda i: (0, 0)),
            pl.BlockSpec((width, piece), lambda i: (0, i)),
            pl.BlockSpec((width, piece), lambda i: (0, i)),
            pl.BlockSpec((piece, width), lambda i: (i, 0)),
        ],
        out_specs=pl.BlockSpec((count, width), lambda i: (0, 0)),
        scratch_shapes=[pltpu.VMEM((count, width), F32)],
        out_shape=jax.ShapeDtypeStruct((count, width), BF16),
        compiler_params=params(40),
        cost_estimate=pl.CostEstimate(
            flops=6 * count * width * inner,
            bytes_accessed=6 * width * inner,
            transcendentals=count * inner,
        ),
    )(rows, gate_weight, up_weight, down_weight)


def shards(
    tokens,
    attn_gain,
    q_weight,
    k_weight,
    v_weight,
    q_gain,
    k_gain,
    out_weight,
    moe_gain,
    expert_ids,
    route_code,
    gate_weight,
    up_weight,
    expert_down_matrix,
):
    exp_count = lax.axis_size("exp")
    ctx_count = lax.axis_size("ctx")
    ctx_place = lax.axis_index("ctx")
    exp_place = lax.axis_index("exp")
    tok_rows, width = tokens.shape
    head = q_gain.shape[0]
    feats = q_weight.shape[1]
    group_size = feats * exp_count // k_weight.shape[1]
    kv_first = exp_place * (feats // head) // group_size * head
    ring = exp_count // 2
    half_rows = tok_rows * ring
    far = exp_place // ring
    near = exp_place % ring
    rings = [list(range(ring)), list(range(ring, exp_count))]
    flip = [(e, (e + ring) % exp_count) for e in range(exp_count)]
    mirror = [(c, ctx_count - 1 - c) for c in range(ctx_count)]

    def over_ring(parts):
        return lax.all_to_all(parts, "exp", 0, 0, tiled=True, axis_index_groups=rings)

    def to_ring(rows):
        spread = jnp.broadcast_to(rows[None], (ring,) + rows.shape)
        return over_ring(spread).reshape(half_rows, width)

    packed = jnp.concatenate(
        [
            q_weight,
            out_weight.T,
            lax.dynamic_slice_in_dim(k_weight, kv_first, head, 1),
            lax.dynamic_slice_in_dim(v_weight, kv_first, head, 1),
        ],
        axis=1,
    )
    weights = lax.all_gather(packed, "ctx", axis=0, tiled=True)
    normal_rows = normed(tokens, attn_gain).astype(BF16)
    half_tile = tok_rows // 2
    mirrored = lax.ppermute(normal_rows[half_tile:], "ctx", mirror)
    worked = jnp.concatenate([normal_rows[:half_tile], mirrored], axis=0)
    flipped = lax.ppermute(worked, "exp", flip)
    own = to_ring(worked)
    flipped, own = lax.optimization_barrier((flipped, own))
    other = to_ring(flipped)
    far_index = far.astype(jnp.int32).reshape(1)
    kv = project(
        kv_kernel,
        ring,
        far_index,
        own,
        other,
        weights,
        feats // head,
        2 * head,
        k_gain,
        (2 * half_rows, 2 * head),
    )
    kv_all = lax.all_gather(kv, "ctx", axis=0, tiled=True)
    queries = project(
        q_kernel, ring, far_index, own, other, weights, 0, feats, q_gain, (2, half_rows, feats)
    )
    cross = [
        (c * exp_count + e, (ctx_count - 1 - c) * exp_count + (e + ring) % exp_count)
        for c in range(ctx_count)
        for e in range(exp_count)
    ]
    ctx_index = ctx_place.astype(jnp.int32).reshape(1)
    shares = []
    for part in range(2):
        sums = attend(ctx_index, queries, kv_all, weights, head, ring, part, 2)
        if part == 0:
            raw, ids, sums = lax.optimization_barrier((tokens, expert_ids, sums))
            partner = lax.ppermute(raw, "exp", flip)
            partner_ids = lax.ppermute(ids, "exp", flip)
        shares.append(jnp.sum(over_ring(sums).astype(F32), axis=0))
    shares = jnp.concatenate(shares, axis=2)
    rounded = shares.astype(BF16).reshape(2, tok_rows, width)
    by_flip = lax.ppermute(rounded[0], "exp", flip)
    by_mirror = lax.ppermute(rounded[1], "ctx", mirror)
    by_cross = lax.ppermute(rounded[1], ("ctx", "exp"), cross)

    def by_side(mine, theirs):
        return jnp.where(far == 0, jnp.stack([mine, theirs]), jnp.stack([theirs, mine]))

    sides = by_side(tokens, partner).reshape(2, 2, half_tile, width)
    sides = sides.swapaxes(0, 1).reshape(2 * tok_rows, width)
    top_count = expert_ids.shape[1]
    capacity = min(tok_rows, 2 * tok_rows * top_count // exp_count)
    places = jnp.arange(exp_count * capacity, dtype=jnp.int32)

    def slots_of(ids, experts):
        flat = ids.reshape(-1)
        one_hot = (flat[:, None] == experts[None, :]).astype(jnp.int32)
        earlier = jnp.cumsum(one_hot, axis=0) - one_hot
        rank = jnp.sum(earlier * one_hot, axis=1)
        known = jnp.sum(one_hot, axis=1) > 0
        slots = jnp.where(known, (flat - experts[0]) * capacity + rank, -1)
        return slots.reshape(tok_rows, top_count)

    near_experts = jnp.arange(ring, dtype=jnp.int32) + far * ring
    both_slots = jnp.stack(
        [slots_of(side, near_experts) for side in by_side(expert_ids, partner_ids)]
    )
    expert_of, rank_of = both_slots // capacity, both_slots % capacity
    side_of = jnp.arange(2, dtype=jnp.int32)[:, None, None]
    rows_of = jnp.where(both_slots < 0, -1, (expert_of * 2 + side_of) * capacity + rank_of)
    rows_of = rows_of.reshape(2, 2, half_tile, top_count).swapaxes(0, 1)
    rows_of = rows_of.reshape(2 * tok_rows, top_count)
    chosen = jnp.any(places[:, None, None] == rows_of[None], axis=-1).astype(BF16)
    mixed_both, sent = pl.pallas_call(
        mix_kernel,
        out_shape=(
            jax.ShapeDtypeStruct(sides.shape, BF16),
            jax.ShapeDtypeStruct((exp_count * capacity, width), BF16),
        ),
        compiler_params=params(40),
    )(
        sides,
        shares[0].reshape(tok_rows, width),
        by_flip,
        by_mirror,
        by_cross,
        moe_gain.reshape(1, -1),
        chosen,
    )
    mixed_both = mixed_both.reshape(2, 2, half_tile, width)
    mixed = lax.dynamic_index_in_dim(mixed_both, far, 1, keepdims=False).reshape(tok_rows, width)
    arrived = over_ring(sent.reshape(ring, 2 * capacity, width)).reshape(-1, width)
    done = run_experts(arrived, gate_weight[0], up_weight[0], expert_down_matrix[0])
    done = done.reshape(ring, 2, capacity, width).swapaxes(0, 1)
    back = lax.all_to_all(
        done.reshape(exp_count, capacity, width), "exp", split_axis=0, concat_axis=0, tiled=True
    ).reshape(exp_count * capacity, width)
    slots = slots_of(expert_ids, jnp.arange(exp_count, dtype=jnp.int32))
    codes = route_code.astype(F32)
    route_weight = codes / jnp.sum(codes, axis=-1, keepdims=True)
    total = mixed.astype(F32)
    for j in range(top_count):
        pick = (slots[:, j : j + 1] == places[None, :]).astype(BF16)
        picked = jnp.dot(pick, back, preferred_element_type=F32)
        total = total + picked * route_weight[:, j : j + 1]
    return total.astype(BF16)


def solution(mesh):
    placed = (
        P(("ctx", "exp"), None),
        P(),
        P("ctx", "exp"),
        P("ctx", None),
        P("ctx", None),
        P(),
        P(),
        P("exp", "ctx"),
        P(),
        P(("ctx", "exp"), None),
        P(("ctx", "exp"), None),
        P("exp", None, None),
        P("exp", None, None),
        P("exp", None, None),
    )
    return jax.shard_map(
        shards, mesh=mesh, in_specs=placed, out_specs=P(("ctx", "exp"), None), check_vma=False
    )
```

```python
import functools
import math

import jax
import jax.numpy as jnp
from jax import lax
from jax.experimental import pallas as pl
from jax.experimental.pallas import tpu as pltpu
from jax.sharding import PartitionSpec as P

F32 = jnp.float32
BF16 = jnp.bfloat16
NT = (((1,), (1,)), ((), ()))
EPS = 1e-06


def normed(values, gain):
    widened = values.astype(F32)
    square = jnp.mean(widened * widened, axis=-1, keepdims=True)
    return widened * lax.rsqrt(square + EPS) * gain.astype(F32)


def params(vmem_mib):
    return pltpu.CompilerParams(vmem_limit_bytes=vmem_mib * 2**20)


def in_runs(values, ring):
    run = values.shape[0] // ring
    for job in range(2):
        yield jnp.concatenate(
            [
                values[near * run + job * run // 2 : near * run + (job + 1) * run // 2]
                for near in range(ring)
            ],
            axis=0,
        )


def kv_kernel(ring, place_ref, own_ref, other_ref, w_ref, gain_ref, out_ref):
    half, head = own_ref.shape[0], gain_ref.shape[1]
    mine = place_ref[0]
    for rows_ref, spot in ((own_ref, mine), (other_ref, 1 - mine)):
        sums = jnp.dot(rows_ref[...], w_ref[...], preferred_element_type=F32)
        for job, part in enumerate(in_runs(sums, ring)):
            keys = normed(part[:, :head], gain_ref[...]).astype(BF16)
            start = job * half + pl.multiple_of(spot * (half // 2), half // 2)
            out_ref[pl.ds(start, half // 2), :head] = keys
            for at in range(0, half // 2, head):
                block = part[at : at + head, head:].T.astype(BF16)
                out_ref[pl.ds(start + at, head), head:] = block


def q_kernel(ring, place_ref, own_ref, other_ref, w_ref, gain_ref, out_ref):
    half, head = own_ref.shape[0], gain_ref.shape[1]
    mine = place_ref[0]
    for rows_ref, spot in ((own_ref, mine), (other_ref, 1 - mine)):
        sums = jnp.dot(rows_ref[...], w_ref[...], preferred_element_type=F32)
        for job, part in enumerate(in_runs(sums, ring)):
            start = pl.multiple_of(spot * (half // 2), half // 2)
            for one in range(w_ref.shape[1] // head):
                cols = slice(one * head, (one + 1) * head)
                out_ref[job, pl.ds(start, half // 2), cols] = normed(
                    part[:, cols], gain_ref[...]
                ).astype(BF16)


def project(kernel, ring, place, own, other, weights, col_block, width, gain, out_shape):
    half, depth = own.shape
    return pl.pallas_call(
        functools.partial(kernel, ring),
        grid_spec=pltpu.PrefetchScalarGridSpec(
            num_scalar_prefetch=1,
            grid=(1,),
            in_specs=[
                pl.BlockSpec((half, depth), lambda i, p: (0, 0)),
                pl.BlockSpec((half, depth), lambda i, p: (0, 0)),
                pl.BlockSpec((depth, width), lambda i, p: (0, col_block)),
                pl.BlockSpec((1, gain.shape[0]), lambda i, p: (0, 0)),
            ],
            out_specs=pl.BlockSpec(out_shape, lambda i, p: (0,) * len(out_shape)),
        ),
        out_shape=jax.ShapeDtypeStruct(out_shape, BF16),
        compiler_params=params(58),
        cost_estimate=pl.CostEstimate(
            flops=4 * half * depth * width, bytes_accessed=8 * 2**20, transcendentals=0
        ),
    )(place, own, other, weights, gain.reshape(1, -1))


def attention_kernel(
    scale, part, place_ref, q_ref, kv_hbm, w_hbm, out_ref, kv_ref, wo_ref, qt_ref, acc_ref, att_ref, sems, wo_sem
):
    ring, jobs, sides, tile, width = out_ref.shape
    half, feats = q_ref.shape[1:]
    head = acc_ref.shape[0]
    heads = feats // head
    devices = ring * sides
    rows = devices * tile
    span = half // devices
    block = 2 * half
    chunks = sems.shape[0]
    ctx = kv_ref.shape[0] // block
    per = ctx // chunks
    place = place_ref[0]
    pair = 4
    cols = pair * rows
    longest = jnp.maximum(place, ctx - 1 - place)

    def chunk_wait(at):
        piece = pl.ds(pl.multiple_of(at * per * block, block), per * block)
        pltpu.make_async_copy(kv_hbm.at[piece], kv_ref.at[piece], sems.at[at]).wait()

    wo_copy = pltpu.make_async_copy(w_hbm.at[:, feats : 2 * feats], wo_ref, wo_sem)
    for at in range(chunks):
        @pl.when(at * per <= longest)
        def _(at=at):
            for one in range(at * per, (at + 1) * per):
                first = pl.ds(one * block, half)
                pltpu.make_async_copy(kv_hbm.at[first], kv_ref.at[first], sems.at[at]).start()
                pltpu.make_async_copy(
                    kv_hbm.at[pl.ds((ctx - 1 - one) * block + half, half)],
                    kv_ref.at[pl.ds(one * block + half, half)],
                    sems.at[at],
                ).start()

    wo_copy.start()

    for job in range(2):
        for one in range(heads):
            picked = jnp.concatenate(
                [
                    q_ref[
                        job,
                        e * span + part * tile : e * span + (part + 1) * tile,
                        one * head : (one + 1) * head,
                    ]
                    for e in range(devices)
                ],
                axis=0,
            )
            qt_ref[job, :, one * rows : (one + 1) * rows] = picked.astype(F32).T.astype(BF16)

    def one_job(turn, carry):
        own = jnp.where(turn == 0, place >= ctx - 1 - place, place < ctx - 1 - place)
        job = jnp.where(own, 0, 1)
        blocks = jnp.where(own, place, ctx - 1 - place)
        groups = heads // pair

        def steps(starts, state, masked=False):
            count = block
            state = list(state)
            items = [(start, group) for start in starts for group in range(groups)]

            def product(item):
                start, group = item
                keys = kv_ref[pl.ds(pl.multiple_of(start, half), count), :head]
                queries = qt_ref[job, :, group * cols : (group + 1) * cols]
                return jnp.dot(keys, queries, preferred_element_type=F32)

            def collect(start, group, weights, decay):
                values = jnp.concatenate(
                    [
                        kv_ref[pl.ds(pl.multiple_of(start + i * head, head), head), head:]
                        for i in range(count // head)
                    ],
                    axis=1,
                )
                spot = slice(group * cols, (group + 1) * cols)
                acc_ref[:, spot] = acc_ref[:, spot] * decay + jnp.dot(
                    values, weights, preferred_element_type=F32
                )

            following = product(items[0])
            waiting = None
            for at, (start, group) in enumerate(items):
                scores = following
                if at + 1 < len(items):
                    following = product(items[at + 1])
                if masked and at // groups == len(starts) - 1:
                    key_at = lax.broadcasted_iota(jnp.int32, scores.shape, 0)
                    col = lax.broadcasted_iota(jnp.int32, scores.shape, 1) % rows
                    row_at = (col // tile * 2 + job) * span + part * tile + col % tile
                    key_at = (key_at % half // span * 2 + key_at // half) * span + key_at % span
                    scores = jnp.where(key_at <= row_at, scores, -1e30)
                before, total = state[2 * group], state[2 * group + 1]
                largest = jnp.maximum(before, jnp.max(scores, axis=0, keepdims=True))
                weights = jnp.exp2((scores - largest) * scale)
                decay = jnp.exp2((before - largest) * scale)
                state[2 * group] = largest
                state[2 * group + 1] = total * decay + jnp.sum(
                    weights.reshape(count // 8, 8, cols), axis=0
                )
                if waiting is not None:
                    collect(*waiting)
                waiting = (start, group, weights.astype(BF16), decay)
            collect(*waiting)
            return tuple(state)

        def arrive(at):
            @pl.when(turn == 0)
            def _():
                chunk_wait(at)

        def whole_chunk(at, state):
            arrive(at)
            return steps([(at * per + i) * block for i in range(per)], state)

        acc_ref[...] = jnp.zeros_like(acc_ref)
        state = (jnp.full((1, cols), -1e30, F32), jnp.zeros((8, cols), F32)) * groups
        full = blocks // per
        state = lax.fori_loop(0, full, whole_chunk, state)
        arrive(full)
        tails = [
            lambda now, left=left: steps(
                [(blocks - left + i) * block for i in range(left + 1)], now, masked=True
            )
            for left in range(per)
        ]
        state = lax.switch(blocks - full * per, tails, state)
        for group in range(groups):
            total = jnp.sum(state[2 * group + 1], axis=0, keepdims=True)
            spot = slice(group * cols, (group + 1) * cols)
            acc_ref[:, spot] = acc_ref[:, spot] / total
        for one in range(heads):
            att_ref[:, one * head : (one + 1) * head] = acc_ref[
                :, one * rows : (one + 1) * rows
            ].T.astype(BF16)

        @pl.when(turn == 0)
        def _():
            wo_copy.wait()

        piece = min(512, width)
        for at in range(0, width, piece):
            sums = lax.dot_general(
                att_ref[...], wo_ref[at : at + piece, :], NT, preferred_element_type=F32
            ).astype(BF16)
            for e in range(devices):
                out_ref[e % ring, job, e // ring, :, at : at + piece] = sums[
                    e * tile : (e + 1) * tile
                ]
        return carry

    lax.fori_loop(0, 2, one_job, 0)


def attend(place, queries, kv, weights, head, ring, part, parts):
    half, feats = queries.shape[1:]
    width = weights.shape[0]
    tile = half // (2 * ring) // parts
    rows = tile * 2 * ring
    ctx = kv.shape[0] // (2 * half)
    chunks = max(1, ctx // 4)
    flops = 8 * kv.shape[0] * rows * feats
    return pl.pallas_call(
        functools.partial(attention_kernel, math.log2(math.e) / math.sqrt(head), part),
        grid_spec=pltpu.PrefetchScalarGridSpec(
            num_scalar_prefetch=1,
            grid=(1,),
            in_specs=[
                pl.BlockSpec((2, half, feats), lambda i, p: (0, 0, 0)),
                pl.BlockSpec(memory_space=pltpu.HBM),
                pl.BlockSpec(memory_space=pltpu.HBM),
            ],
            out_specs=pl.BlockSpec((ring, 2, 2, tile, width), lambda i, p: (0,) * 5),
            scratch_shapes=[
                pltpu.VMEM(kv.shape, BF16),
                pltpu.VMEM((width, feats), BF16),
                pltpu.VMEM((2, head, rows * feats // head), BF16),
                pltpu.VMEM((head, rows * feats // head), F32),
                pltpu.VMEM((rows, feats), BF16),
                pltpu.SemaphoreType.DMA((chunks,)),
                pltpu.SemaphoreType.DMA,
            ],
        ),
        out_shape=jax.ShapeDtypeStruct((ring, 2, 2, tile, width), BF16),
        compiler_params=params(58),
        cost_estimate=pl.CostEstimate(
            flops=flops, bytes_accessed=16 * 2**20, transcendentals=flops // 512
        ),
    )(place, queries, kv, weights)


def mix_kernel(*refs):
    *part_refs, gain_ref, chosen_ref, mixed_ref, sent_ref = refs
    parts = len(part_refs) // 4
    for part in range(parts):
        kept_ref, flip_ref, mirror_ref, cross_ref = part_refs[4 * part : 4 * part + 4]
        sides, tile, width = kept_ref.shape
        sums = (
            kept_ref[...] + flip_ref[...].astype(F32),
            mirror_ref[...].astype(F32) + cross_ref[...].astype(F32),
        )
        for job in range(2):
            for side in range(sides):
                start = ((job * sides + side) * parts + part) * tile
                mixed_ref[start : start + tile] = sums[job][side].astype(BF16)
    rows = normed(mixed_ref[...], gain_ref[...]).astype(BF16)
    sent_ref[...] = jnp.dot(chosen_ref[...], rows, preferred_element_type=F32).astype(BF16)


def expert_kernel(rows_ref, gate_ref, up_ref, down_ref, out_ref, total_ref):
    step = pl.program_id(0)
    gate = jnp.dot(rows_ref[...], gate_ref[...], preferred_element_type=F32)
    up = jnp.dot(rows_ref[...], up_ref[...], preferred_element_type=F32)
    hidden = (gate / (1.0 + jnp.exp(-gate)) * up).astype(BF16)
    share = jnp.dot(hidden, down_ref[...], preferred_element_type=F32)

    @pl.when(step == 0)
    def _():
        total_ref[...] = share

    @pl.when(step > 0)
    def _():
        total_ref[...] += share

    @pl.when(step == pl.num_programs(0) - 1)
    def _():
        out_ref[...] = total_ref[...].astype(BF16)


def run_experts(rows, gate_weight, up_weight, down_weight):
    count, width = rows.shape
    inner = gate_weight.shape[1]
    piece = math.gcd(inner, 256)
    return pl.pallas_call(
        expert_kernel,
        grid=(inner // piece,),
        in_specs=[
            pl.BlockSpec((count, width), lambda i: (0, 0)),
            pl.BlockSpec((width, piece), lambda i: (0, i)),
            pl.BlockSpec((width, piece), lambda i: (0, i)),
            pl.BlockSpec((piece, width), lambda i: (i, 0)),
        ],
        out_specs=pl.BlockSpec((count, width), lambda i: (0, 0)),
        scratch_shapes=[pltpu.VMEM((count, width), F32)],
        out_shape=jax.ShapeDtypeStruct((count, width), BF16),
        compiler_params=params(58),
        cost_estimate=pl.CostEstimate(
            flops=6 * count * width * inner,
            bytes_accessed=6 * width * inner,
            transcendentals=count * inner,
        ),
    )(rows, gate_weight, up_weight, down_weight)


def combine_kernel(back_ref, rows_ref, weight_ref, base_ref, out_ref):
    total = base_ref[...].astype(F32)
    places = lax.broadcasted_iota(jnp.int32, (rows_ref.shape[0], back_ref.shape[0]), 1)
    for j in range(rows_ref.shape[1]):
        pick = (rows_ref[:, j : j + 1] == places).astype(F32).astype(BF16)
        picked = jnp.dot(pick, back_ref[...], preferred_element_type=F32)
        total = total + picked * weight_ref[:, j : j + 1]
    out_ref[...] = total.astype(out_ref.dtype)


def combine(back, rows, weight, base, dtype):
    return pl.pallas_call(
        combine_kernel,
        out_shape=jax.ShapeDtypeStruct(base.shape, dtype),
        compiler_params=params(40),
        cost_estimate=pl.CostEstimate(
            flops=4 * rows.shape[0] * back.size, bytes_accessed=2 * back.size, transcendentals=0
        ),
    )(back, rows, weight, base)


def shards(
    tokens,
    attn_gain,
    q_weight,
    k_weight,
    v_weight,
    q_gain,
    k_gain,
    out_weight,
    moe_gain,
    expert_ids,
    route_code,
    gate_weight,
    up_weight,
    expert_down_matrix,
):
    exp_count = lax.axis_size("exp")
    ctx_count = lax.axis_size("ctx")
    ctx_place = lax.axis_index("ctx")
    exp_place = lax.axis_index("exp")
    tok_rows, width = tokens.shape
    head = q_gain.shape[0]
    feats = q_weight.shape[1]
    group_size = feats * exp_count // k_weight.shape[1]
    kv_first = exp_place * (feats // head) // group_size * head
    ring = exp_count // 2
    half_rows = tok_rows * ring
    far = exp_place // ring
    near = exp_place % ring
    rings = [list(range(ring)), list(range(ring, exp_count))]
    flip = [(e, (e + ring) % exp_count) for e in range(exp_count)]
    mirror = [(c, ctx_count - 1 - c) for c in range(ctx_count)]

    def over_ring(parts):
        return lax.all_to_all(parts, "exp", 0, 0, tiled=True, axis_index_groups=rings)

    def to_ring(rows):
        spread = jnp.broadcast_to(rows[None], (ring,) + rows.shape)
        return over_ring(spread).reshape(half_rows, width)

    packed = jnp.concatenate(
        [
            q_weight,
            out_weight.T,
            lax.dynamic_slice_in_dim(k_weight, kv_first, head, 1),
            lax.dynamic_slice_in_dim(v_weight, kv_first, head, 1),
        ],
        axis=1,
    )
    weights = lax.all_gather(packed, "ctx", axis=0, tiled=True)
    half_tile = tok_rows // 2
    mirrored = lax.ppermute(tokens[half_tile:], "ctx", mirror)
    raw = jnp.concatenate([tokens[:half_tile], mirrored], axis=0)
    worked = normed(raw, attn_gain).astype(BF16)
    routes = jnp.concatenate([expert_ids, route_code], axis=1)
    partner_routes = lax.ppermute(routes, "exp", flip)
    flipped = lax.ppermute(worked, "exp", flip)
    own = to_ring(worked)
    flipped, own = lax.optimization_barrier((flipped, own))
    other = to_ring(flipped)
    far_index = far.astype(jnp.int32).reshape(1)
    kv = project(
        kv_kernel,
        ring,
        far_index,
        own,
        other,
        weights,
        feats // head,
        2 * head,
        k_gain,
        (2 * half_rows, 2 * head),
    )
    kv_all = lax.all_gather(kv, "ctx", axis=0, tiled=True)
    queries = project(
        q_kernel, ring, far_index, own, other, weights, 0, feats, q_gain, (2, half_rows, feats)
    )
    cross = [
        (c * exp_count + e, (ctx_count - 1 - c) * exp_count + (e + ring) % exp_count)
        for c in range(ctx_count)
        for e in range(exp_count)
    ]
    ctx_index = ctx_place.astype(jnp.int32).reshape(1)
    mine = (jnp.arange(2) == far)[None, :, None, None]
    residual = raw.reshape(2, 1, 2, half_tile // 2, width)
    mixed_parts = []
    rounded = None
    for part in range(2):
        sums = attend(ctx_index, queries, kv_all, weights, head, ring, part, 2)
        if part:
            sums, rounded = lax.optimization_barrier((sums, rounded))
        shares = jnp.sum(over_ring(sums).astype(F32), axis=0)
        shares = shares + jnp.where(mine, residual[:, :, part].astype(F32), 0.0)
        rounded = shares.astype(BF16)
        mixed_parts += [
            shares[0],
            lax.ppermute(rounded[0], "exp", flip),
            lax.ppermute(rounded[1], "ctx", mirror),
            lax.ppermute(rounded[1], ("ctx", "exp"), cross),
        ]

    def by_side(mine, theirs):
        return jnp.where(far == 0, jnp.stack([mine, theirs]), jnp.stack([theirs, mine]))

    top_count = expert_ids.shape[1]
    capacity = min(tok_rows, 2 * tok_rows * top_count // exp_count)
    places = jnp.arange(exp_count * capacity, dtype=jnp.int32)

    def slots_of(ids, experts):
        flat = ids.reshape(-1)
        one_hot = (flat[:, None] == experts[None, :]).astype(jnp.int32)
        earlier = jnp.cumsum(one_hot, axis=0) - one_hot
        rank = jnp.sum(earlier * one_hot, axis=1)
        known = jnp.sum(one_hot, axis=1) > 0
        slots = jnp.where(known, (flat - experts[0]) * capacity + rank, -1)
        return slots.reshape(tok_rows, top_count)

    near_experts = jnp.arange(ring, dtype=jnp.int32) + far * ring
    both_routes = by_side(routes, partner_routes)
    both_slots = jnp.stack([slots_of(side[:, :top_count], near_experts) for side in both_routes])
    expert_of, rank_of = both_slots // capacity, both_slots % capacity
    side_of = jnp.arange(2, dtype=jnp.int32)[:, None, None]
    rows_of = jnp.where(both_slots < 0, -1, (expert_of * 2 + side_of) * capacity + rank_of)
    sorted_rows = rows_of.reshape(2, 2, half_tile, top_count).swapaxes(0, 1)
    sorted_rows = sorted_rows.reshape(2 * tok_rows, top_count)
    chosen = jnp.any(places[:, None, None] == sorted_rows[None], axis=-1).astype(BF16)
    codes = both_routes[:, :, top_count:].astype(F32)
    route_weight = codes / jnp.sum(codes, axis=-1, keepdims=True)
    mixed_both, sent = pl.pallas_call(
        mix_kernel,
        out_shape=(
            jax.ShapeDtypeStruct((2 * tok_rows, width), BF16),
            jax.ShapeDtypeStruct((exp_count * capacity, width), BF16),
        ),
        compiler_params=params(40),
    )(*mixed_parts, moe_gain.reshape(1, -1), chosen)
    mixed_both = mixed_both.reshape(2, 2, half_tile, width)
    mixed = lax.dynamic_index_in_dim(mixed_both, far, 1, keepdims=False).reshape(tok_rows, width)
    arrived = over_ring(sent.reshape(ring, 2 * capacity, width)).reshape(-1, width)
    done = run_experts(arrived, gate_weight[0], up_weight[0], expert_down_matrix[0])
    back = over_ring(done.reshape(ring, 2 * capacity, width)).reshape(-1, width)
    theirs, mine = (
        [lax.dynamic_index_in_dim(a, side, 0, keepdims=False) for a in (rows_of, route_weight)]
        for side in (1 - far, far)
    )
    given = combine(back, *theirs, jnp.zeros((tok_rows, width), F32), BF16)
    returned = lax.ppermute(given, "exp", flip)
    total = combine(back, *mine, mixed, F32)
    return (total + returned.astype(F32)).astype(BF16)


def solution(mesh):
    placed = (
        P(("ctx", "exp"), None),
        P(),
        P("ctx", "exp"),
        P("ctx", None),
        P("ctx", None),
        P(),
        P(),
        P("exp", "ctx"),
        P(),
        P(("ctx", "exp"), None),
        P(("ctx", "exp"), None),
        P("exp", None, None),
        P("exp", None, None),
        P("exp", None, None),
    )
    return jax.shard_map(
        shards, mesh=mesh, in_specs=placed, out_specs=P(("ctx", "exp"), None), check_vma=False
    )
```

```python
import functools
import math

import jax
import jax.numpy as jnp
from jax import lax
from jax.experimental import pallas as pl
from jax.experimental.pallas import tpu as pltpu
from jax.sharding import PartitionSpec as P

F32 = jnp.float32
BF16 = jnp.bfloat16
NT = (((1,), (1,)), ((), ()))
EPS = 1e-06


def normed(values, gain):
    widened = values.astype(F32)
    square = jnp.mean(widened * widened, axis=-1, keepdims=True)
    return widened * lax.rsqrt(square + EPS) * gain.astype(F32)


def params(vmem_mib):
    return pltpu.CompilerParams(vmem_limit_bytes=vmem_mib * 2**20)


def in_runs(values, ring):
    run = values.shape[0] // ring
    for job in range(2):
        yield jnp.concatenate(
            [
                values[near * run + job * run // 2 : near * run + (job + 1) * run // 2]
                for near in range(ring)
            ],
            axis=0,
        )


def kv_kernel(ring, place_ref, own_ref, other_ref, w_ref, gain_ref, out_ref):
    half, head = own_ref.shape[0], gain_ref.shape[1]
    mine = place_ref[0]
    for rows_ref, spot in ((own_ref, mine), (other_ref, 1 - mine)):
        sums = jnp.dot(rows_ref[...], w_ref[...], preferred_element_type=F32)
        for job, part in enumerate(in_runs(sums, ring)):
            keys = normed(part[:, :head], gain_ref[...]).astype(BF16)
            start = job * half + pl.multiple_of(spot * (half // 2), half // 2)
            out_ref[pl.ds(start, half // 2), :head] = keys
            for at in range(0, half // 2, head):
                block = part[at : at + head, head:].T.astype(BF16)
                out_ref[pl.ds(start + at, head), head:] = block


def q_kernel(ring, place_ref, own_ref, other_ref, w_ref, gain_ref, out_ref):
    half, head = own_ref.shape[0], gain_ref.shape[1]
    mine = place_ref[0]
    for rows_ref, spot in ((own_ref, mine), (other_ref, 1 - mine)):
        sums = jnp.dot(rows_ref[...], w_ref[...], preferred_element_type=F32)
        for job, part in enumerate(in_runs(sums, ring)):
            start = pl.multiple_of(spot * (half // 2), half // 2)
            for one in range(w_ref.shape[1] // head):
                cols = slice(one * head, (one + 1) * head)
                out_ref[job, pl.ds(start, half // 2), cols] = normed(
                    part[:, cols], gain_ref[...]
                ).astype(BF16)


def project(kernel, ring, place, own, other, weights, col_block, width, gain, out_shape):
    half, depth = own.shape
    return pl.pallas_call(
        functools.partial(kernel, ring),
        grid_spec=pltpu.PrefetchScalarGridSpec(
            num_scalar_prefetch=1,
            grid=(1,),
            in_specs=[
                pl.BlockSpec((half, depth), lambda i, p: (0, 0)),
                pl.BlockSpec((half, depth), lambda i, p: (0, 0)),
                pl.BlockSpec((depth, width), lambda i, p: (0, col_block)),
                pl.BlockSpec((1, gain.shape[0]), lambda i, p: (0, 0)),
            ],
            out_specs=pl.BlockSpec(out_shape, lambda i, p: (0,) * len(out_shape)),
        ),
        out_shape=jax.ShapeDtypeStruct(out_shape, BF16),
        compiler_params=params(58),
        cost_estimate=pl.CostEstimate(
            flops=4 * half * depth * width, bytes_accessed=8 * 2**20, transcendentals=0
        ),
    )(place, own, other, weights, gain.reshape(1, -1))


def attention_kernel(
    scale, part, place_ref, q_ref, kv_hbm, w_hbm, out_ref, kv_ref, wo_ref, qt_ref, acc_ref, att_ref, sems, wo_sem
):
    ring, jobs, sides, tile, width = out_ref.shape
    half, feats = q_ref.shape[1:]
    head = acc_ref.shape[0]
    heads = feats // head
    devices = ring * sides
    rows = devices * tile
    span = half // devices
    block = 2 * half
    chunks = sems.shape[1]
    ctx = kv_ref.shape[0]
    per = ctx // chunks
    place = place_ref[0]
    pair = 4
    cols = pair * rows
    longest = jnp.maximum(place, ctx - 1 - place)

    def chunk_copies(at):
        for job, first in enumerate((at * per, ctx - (at + 1) * per)):
            piece = (pl.ds(first, per), job)
            yield pltpu.make_async_copy(kv_hbm.at[piece], kv_ref.at[piece], sems.at[job, at])

    wo_copy = pltpu.make_async_copy(w_hbm.at[:, feats : 2 * feats], wo_ref, wo_sem)
    for at in range(chunks):
        @pl.when(at * per <= longest)
        def _(at=at):
            for copy in chunk_copies(at):
                copy.start()

    wo_copy.start()

    for job in range(2):
        for one in range(heads):
            picked = jnp.concatenate(
                [
                    q_ref[
                        job,
                        e * span + part * tile : e * span + (part + 1) * tile,
                        one * head : (one + 1) * head,
                    ]
                    for e in range(devices)
                ],
                axis=0,
            )
            qt_ref[job, :, one * rows : (one + 1) * rows] = picked.astype(F32).T.astype(BF16)

    def one_job(turn, carry):
        own = jnp.where(turn == 0, place >= ctx - 1 - place, place < ctx - 1 - place)
        job = jnp.where(own, 0, 1)
        blocks = jnp.where(own, place, ctx - 1 - place)
        groups = heads // pair

        def steps(starts, state, masked=False):
            count = block
            state = list(state)
            items = [(start, group) for start in starts for group in range(groups)]

            def product(item):
                start, group = item
                keys = jnp.concatenate(
                    [kv_ref[start, 0, :, :head], kv_ref[ctx - 1 - start, 1, :, :head]], axis=0
                )
                queries = qt_ref[job, :, group * cols : (group + 1) * cols]
                return jnp.dot(keys, queries, preferred_element_type=F32)

            def collect(start, group, weights, decay):
                values = jnp.concatenate(
                    [
                        kv_ref[spot, job, i * head : (i + 1) * head, head:]
                        for job, spot in enumerate((start, ctx - 1 - start))
                        for i in range(half // head)
                    ],
                    axis=1,
                )
                spot = slice(group * cols, (group + 1) * cols)
                acc_ref[:, spot] = acc_ref[:, spot] * decay + jnp.dot(
                    values, weights, preferred_element_type=F32
                )

            following = product(items[0])
            waiting = None
            for at, (start, group) in enumerate(items):
                scores = following
                if at + 1 < len(items):
                    following = product(items[at + 1])
                if masked and at // groups == len(starts) - 1:
                    key_at = lax.broadcasted_iota(jnp.int32, scores.shape, 0)
                    col = lax.broadcasted_iota(jnp.int32, scores.shape, 1) % rows
                    row_at = (col // tile * 2 + job) * span + part * tile + col % tile
                    key_at = (key_at % half // span * 2 + key_at // half) * span + key_at % span
                    scores = jnp.where(key_at <= row_at, scores, -1e30)
                before, total = state[2 * group], state[2 * group + 1]
                largest = jnp.maximum(before, jnp.max(scores, axis=0, keepdims=True))
                weights = jnp.exp2((scores - largest) * scale)
                decay = jnp.exp2((before - largest) * scale)
                state[2 * group] = largest
                state[2 * group + 1] = total * decay + jnp.sum(
                    weights.reshape(count // 8, 8, cols), axis=0
                )
                if waiting is not None:
                    collect(*waiting)
                waiting = (start, group, weights.astype(BF16), decay)
            collect(*waiting)
            return tuple(state)

        def arrive(at):
            @pl.when(turn == 0)
            def _():
                for copy in chunk_copies(at):
                    copy.wait()

        def whole_chunk(at, state):
            arrive(at)
            return steps([at * per + i for i in range(per)], state)

        acc_ref[...] = jnp.zeros_like(acc_ref)
        state = (jnp.full((1, cols), -1e30, F32), jnp.zeros((8, cols), F32)) * groups
        full = blocks // per
        state = lax.fori_loop(0, full, whole_chunk, state)
        arrive(full)
        tails = [
            lambda now, left=left: steps(
                [blocks - left + i for i in range(left + 1)], now, masked=True
            )
            for left in range(per)
        ]
        state = lax.switch(blocks - full * per, tails, state)
        for group in range(groups):
            total = jnp.sum(state[2 * group + 1], axis=0, keepdims=True)
            spot = slice(group * cols, (group + 1) * cols)
            acc_ref[:, spot] = acc_ref[:, spot] / total
        for one in range(heads):
            att_ref[:, one * head : (one + 1) * head] = acc_ref[
                :, one * rows : (one + 1) * rows
            ].T.astype(BF16)

        @pl.when(turn == 0)
        def _():
            wo_copy.wait()

        piece = min(512, width)
        for at in range(0, width, piece):
            sums = lax.dot_general(
                att_ref[...], wo_ref[at : at + piece, :], NT, preferred_element_type=F32
            ).astype(BF16)
            for e in range(devices):
                out_ref[e % ring, job, e // ring, :, at : at + piece] = sums[
                    e * tile : (e + 1) * tile
                ]
        return carry

    lax.fori_loop(0, 2, one_job, 0)


def attend(place, queries, kv, weights, head, ring, part, parts):
    half, feats = queries.shape[1:]
    width = weights.shape[0]
    tile = half // (2 * ring) // parts
    rows = tile * 2 * ring
    ctx = kv.shape[0] // (2 * half)
    kv = kv.reshape(ctx, 2, half, kv.shape[1])
    chunks = max(1, ctx // 4)
    flops = 16 * ctx * half * rows * feats
    return pl.pallas_call(
        functools.partial(attention_kernel, math.log2(math.e) / math.sqrt(head), part),
        grid_spec=pltpu.PrefetchScalarGridSpec(
            num_scalar_prefetch=1,
            grid=(1,),
            in_specs=[
                pl.BlockSpec((2, half, feats), lambda i, p: (0, 0, 0)),
                pl.BlockSpec(memory_space=pltpu.HBM),
                pl.BlockSpec(memory_space=pltpu.HBM),
            ],
            out_specs=pl.BlockSpec((ring, 2, 2, tile, width), lambda i, p: (0,) * 5),
            scratch_shapes=[
                pltpu.VMEM(kv.shape, BF16),
                pltpu.VMEM((width, feats), BF16),
                pltpu.VMEM((2, head, rows * feats // head), BF16),
                pltpu.VMEM((head, rows * feats // head), F32),
                pltpu.VMEM((rows, feats), BF16),
                pltpu.SemaphoreType.DMA((2, chunks)),
                pltpu.SemaphoreType.DMA,
            ],
        ),
        out_shape=jax.ShapeDtypeStruct((ring, 2, 2, tile, width), BF16),
        compiler_params=params(58),
        cost_estimate=pl.CostEstimate(
            flops=flops, bytes_accessed=16 * 2**20, transcendentals=flops // 512
        ),
    )(place, queries, kv, weights)


def mix_kernel(*refs):
    *part_refs, gain_ref, chosen_ref, mixed_ref, sent_ref = refs
    parts = len(part_refs) // 4
    for part in range(parts):
        kept_ref, flip_ref, mirror_ref, cross_ref = part_refs[4 * part : 4 * part + 4]
        sides, tile, width = kept_ref.shape
        sums = (
            kept_ref[...] + flip_ref[...].astype(F32),
            mirror_ref[...].astype(F32) + cross_ref[...].astype(F32),
        )
        for job in range(2):
            for side in range(sides):
                start = ((job * sides + side) * parts + part) * tile
                mixed_ref[start : start + tile] = sums[job][side].astype(BF16)
    rows = normed(mixed_ref[...], gain_ref[...]).astype(BF16)
    sent_ref[...] = jnp.dot(chosen_ref[...], rows, preferred_element_type=F32).astype(BF16)


def expert_kernel(
    place_ref, rows_ref, gate_hbm, up_hbm, down_hbm, mine_ref, theirs_ref,
    gate_ref, up_ref, down_ref, total_ref, sems,
):
    count, width = rows_ref.shape
    pieces = sems.shape[1]
    copies = []
    for kind, (source, target) in enumerate(
        ((gate_hbm, gate_ref), (up_hbm, up_ref), (down_hbm, down_ref))
    ):
        step = target.shape[0] // pieces
        copies.append(
            [
                pltpu.make_async_copy(
                    source.at[pl.ds(at * step, step)],
                    target.at[pl.ds(at * step, step)],
                    sems.at[kind, at],
                )
                for at in range(pieces)
            ]
        )
    order = [copies[kind][at] for at in range(pieces) for kind in range(2)] + copies[2]
    ahead = 6
    for copy in order[:ahead]:
        copy.start()

    def arrive(at):
        order[at].wait()
        if at + ahead < len(order):
            order[at + ahead].start()

    step = width // pieces
    gate = up = 0.0
    for at in range(pieces):
        part = slice(at * step, (at + 1) * step)
        arrive(2 * at)
        gate += jnp.dot(rows_ref[:, part], gate_ref[part], preferred_element_type=F32)
        arrive(2 * at + 1)
        up += jnp.dot(rows_ref[:, part], up_ref[part], preferred_element_type=F32)
    hidden = (gate / (1.0 + jnp.exp(-gate)) * up).astype(BF16)
    for at in range(2 * pieces, 3 * pieces):
        arrive(at)
    total_ref[...] = jnp.dot(hidden, down_ref[...], preferred_element_type=F32)
    capacity = mine_ref.shape[1]
    for near in range(mine_ref.shape[0]):
        for target, side in ((mine_ref, place_ref[0]), (theirs_ref, 1 - place_ref[0])):
            start = pl.multiple_of((near * 2 + side) * capacity, capacity)
            target[near] = total_ref[pl.ds(start, capacity)].astype(BF16)


def run_experts(place, rows, gate_weight, up_weight, down_weight, ring):
    count, width = rows.shape
    inner = gate_weight.shape[1]
    pieces = 4
    shape = (ring, count // ring // 2, width)
    hbm = pl.BlockSpec(memory_space=pltpu.HBM)
    whole = pl.BlockSpec(shape, lambda i, p: (0, 0, 0))
    return pl.pallas_call(
        expert_kernel,
        grid_spec=pltpu.PrefetchScalarGridSpec(
            num_scalar_prefetch=1,
            grid=(1,),
            in_specs=[pl.BlockSpec((count, width), lambda i, p: (0, 0)), hbm, hbm, hbm],
            out_specs=(whole, whole),
            scratch_shapes=[
                pltpu.VMEM((width, inner), BF16),
                pltpu.VMEM((width, inner), BF16),
                pltpu.VMEM((inner, width), BF16),
                pltpu.VMEM((count, width), F32),
                pltpu.SemaphoreType.DMA((3, pieces)),
            ],
        ),
        out_shape=(jax.ShapeDtypeStruct(shape, BF16),) * 2,
        compiler_params=params(58),
        cost_estimate=pl.CostEstimate(
            flops=6 * count * width * inner,
            bytes_accessed=6 * width * inner,
            transcendentals=count * inner,
        ),
    )(place, rows, gate_weight, up_weight, down_weight)


def combine_kernel(back_ref, rows_ref, weight_ref, base_ref, out_ref):
    total = base_ref[...].astype(F32)
    places = lax.broadcasted_iota(jnp.int32, (rows_ref.shape[0], back_ref.shape[0]), 1)
    for j in range(rows_ref.shape[1]):
        pick = (rows_ref[:, j : j + 1] == places).astype(F32).astype(BF16)
        picked = jnp.dot(pick, back_ref[...], preferred_element_type=F32)
        total = total + picked * weight_ref[:, j : j + 1]
    out_ref[...] = total.astype(out_ref.dtype)


def combine(back, rows, weight, base, dtype):
    return pl.pallas_call(
        combine_kernel,
        out_shape=jax.ShapeDtypeStruct(base.shape, dtype),
        compiler_params=params(40),
        cost_estimate=pl.CostEstimate(
            flops=4 * rows.shape[0] * back.size, bytes_accessed=2 * back.size, transcendentals=0
        ),
    )(back, rows, weight, base)


def shards(
    tokens,
    attn_gain,
    q_weight,
    k_weight,
    v_weight,
    q_gain,
    k_gain,
    out_weight,
    moe_gain,
    expert_ids,
    route_code,
    gate_weight,
    up_weight,
    expert_down_matrix,
):
    exp_count = lax.axis_size("exp")
    ctx_count = lax.axis_size("ctx")
    ctx_place = lax.axis_index("ctx")
    exp_place = lax.axis_index("exp")
    tok_rows, width = tokens.shape
    head = q_gain.shape[0]
    feats = q_weight.shape[1]
    group_size = feats * exp_count // k_weight.shape[1]
    kv_first = exp_place * (feats // head) // group_size * head
    ring = exp_count // 2
    half_rows = tok_rows * ring
    far = exp_place // ring
    near = exp_place % ring
    rings = [list(range(ring)), list(range(ring, exp_count))]
    flip = [(e, (e + ring) % exp_count) for e in range(exp_count)]
    mirror = [(c, ctx_count - 1 - c) for c in range(ctx_count)]

    def over_ring(parts):
        return lax.all_to_all(parts, "exp", 0, 0, tiled=True, axis_index_groups=rings)

    def to_ring(rows):
        spread = jnp.broadcast_to(rows[None], (ring,) + rows.shape)
        return over_ring(spread).reshape(half_rows, width)

    packed = jnp.concatenate(
        [
            q_weight,
            out_weight.T,
            lax.dynamic_slice_in_dim(k_weight, kv_first, head, 1),
            lax.dynamic_slice_in_dim(v_weight, kv_first, head, 1),
        ],
        axis=1,
    )
    weights = lax.all_gather(packed, "ctx", axis=0, tiled=True)
    half_tile = tok_rows // 2
    mirrored = lax.ppermute(tokens[half_tile:], "ctx", mirror)
    raw = jnp.concatenate([tokens[:half_tile], mirrored], axis=0)
    worked = normed(raw, attn_gain).astype(BF16)
    routes = jnp.concatenate([expert_ids, route_code], axis=1)
    partner_routes = lax.ppermute(routes, "exp", flip)
    flipped = lax.ppermute(worked, "exp", flip)
    own = to_ring(worked)
    flipped, own = lax.optimization_barrier((flipped, own))
    other = to_ring(flipped)
    far_index = far.astype(jnp.int32).reshape(1)
    kv = project(
        kv_kernel,
        ring,
        far_index,
        own,
        other,
        weights,
        feats // head,
        2 * head,
        k_gain,
        (2 * half_rows, 2 * head),
    )
    kv_all = lax.all_gather(kv, "ctx", axis=0, tiled=True)
    queries = project(
        q_kernel, ring, far_index, own, other, weights, 0, feats, q_gain, (2, half_rows, feats)
    )
    cross = [
        (c * exp_count + e, (ctx_count - 1 - c) * exp_count + (e + ring) % exp_count)
        for c in range(ctx_count)
        for e in range(exp_count)
    ]
    ctx_index = ctx_place.astype(jnp.int32).reshape(1)
    mine = (jnp.arange(2) == far)[None, :, None, None]
    residual = raw.reshape(2, 1, 2, half_tile // 2, width)
    mixed_parts = []
    rounded = None
    for part in range(2):
        sums = attend(ctx_index, queries, kv_all, weights, head, ring, part, 2)
        if part:
            sums, rounded = lax.optimization_barrier((sums, rounded))
        shares = jnp.sum(over_ring(sums).astype(F32), axis=0)
        shares = shares + jnp.where(mine, residual[:, :, part].astype(F32), 0.0)
        rounded = shares.astype(BF16)
        mixed_parts += [
            shares[0],
            lax.ppermute(rounded[0], "exp", flip),
            lax.ppermute(rounded[1], "ctx", mirror),
            lax.ppermute(rounded[1], ("ctx", "exp"), cross),
        ]

    def by_side(mine, theirs):
        return jnp.where(far == 0, jnp.stack([mine, theirs]), jnp.stack([theirs, mine]))

    top_count = expert_ids.shape[1]
    capacity = min(tok_rows, 2 * tok_rows * top_count // exp_count)
    places = jnp.arange(exp_count * capacity, dtype=jnp.int32)

    def slots_of(ids, experts):
        flat = ids.reshape(-1)
        one_hot = (flat[:, None] == experts[None, :]).astype(jnp.int32)
        earlier = jnp.cumsum(one_hot, axis=0) - one_hot
        rank = jnp.sum(earlier * one_hot, axis=1)
        known = jnp.sum(one_hot, axis=1) > 0
        slots = jnp.where(known, (flat - experts[0]) * capacity + rank, -1)
        return slots.reshape(tok_rows, top_count)

    near_experts = jnp.arange(ring, dtype=jnp.int32) + far * ring
    both_routes = by_side(routes, partner_routes)
    both_slots = jnp.stack([slots_of(side[:, :top_count], near_experts) for side in both_routes])
    expert_of, rank_of = both_slots // capacity, both_slots % capacity
    side_of = jnp.arange(2, dtype=jnp.int32)[:, None, None]
    rows_of = jnp.where(both_slots < 0, -1, (expert_of * 2 + side_of) * capacity + rank_of)
    sorted_rows = rows_of.reshape(2, 2, half_tile, top_count).swapaxes(0, 1)
    sorted_rows = sorted_rows.reshape(2 * tok_rows, top_count)
    chosen = jnp.any(places[:, None, None] == sorted_rows[None], axis=-1).astype(BF16)
    codes = both_routes[:, :, top_count:].astype(F32)
    route_weight = codes / jnp.sum(codes, axis=-1, keepdims=True)
    mixed_both, sent = pl.pallas_call(
        mix_kernel,
        out_shape=(
            jax.ShapeDtypeStruct((2 * tok_rows, width), BF16),
            jax.ShapeDtypeStruct((exp_count * capacity, width), BF16),
        ),
        compiler_params=params(40),
    )(*mixed_parts, moe_gain.reshape(1, -1), chosen)
    mixed_both = mixed_both.reshape(2, 2, half_tile, width)
    mixed = lax.dynamic_index_in_dim(mixed_both, far, 1, keepdims=False).reshape(tok_rows, width)
    arrived = over_ring(sent.reshape(ring, 2 * capacity, width)).reshape(-1, width)
    own_done, far_done = run_experts(
        far_index, arrived, gate_weight[0], up_weight[0], expert_down_matrix[0], ring
    )
    theirs, mine = (
        [lax.dynamic_index_in_dim(a, side, 0, keepdims=False) for a in (both_slots, route_weight)]
        for side in (1 - far, far)
    )
    far_back = over_ring(far_done).reshape(-1, width)
    given = combine(far_back, *theirs, jnp.zeros((tok_rows, width), F32), BF16)
    returned = lax.ppermute(given, "exp", flip)
    given, own_done = lax.optimization_barrier((given, own_done))
    own_back = over_ring(own_done).reshape(-1, width)
    total = combine(own_back, *mine, mixed, F32)
    return (total + returned.astype(F32)).astype(BF16)


def solution(mesh):
    placed = (
        P(("ctx", "exp"), None),
        P(),
        P("ctx", "exp"),
        P("ctx", None),
        P("ctx", None),
        P(),
        P(),
        P("exp", "ctx"),
        P(),
        P(("ctx", "exp"), None),
        P(("ctx", "exp"), None),
        P("exp", None, None),
        P("exp", None, None),
        P("exp", None, None),
    )
    return jax.shard_map(
        shards, mesh=mesh, in_specs=placed, out_specs=P(("ctx", "exp"), None), check_vma=False
    )
```
